512 devices in a mesh: expert: 64 (over x, z, core), replica: 8 (over y).
Axes of the slice: x: 4, y: 8, z: 8, core: 2. Of those that a mesh axis runs over, the one named last changes fastest.
Arguments:
- tokens: bfloat16 [768, 3584], P('expert', 'replica'), may hold values from -6 to 6
- expert_ids: int32 [768, 8], P('expert'), may hold values from 0 to 31, all different within a row; in each aligned block of 12 rows (0 to 11, 12 to 23, ...) at most 4 rows name the same one
- gate_values: float32 [768, 8], P('expert'), may hold values from 0.1 to 0.6
- gate_weight: bfloat16 [64, 512, 3584], P('expert', 'replica'), may hold values from -0.09375 to 0.09375
- up_weight: bfloat16 [64, 512, 3584], P('expert', 'replica'), may hold values from -0.09375 to 0.09375
- down_weight: bfloat16 [64, 512, 3584], P('expert', None, 'replica'), may hold values from -0.1875 to 0.1875
- out_grad: bfloat16 [768, 3584], P('expert', 'replica'), may hold values from -1.5 to 1.5
Outputs:
- moe_out: bfloat16 [768, 3584], P('expert', 'replica')
- token_grad: bfloat16 [768, 3584], P('expert', 'replica')
- gate_grad: bfloat16 [64, 512, 3584], P('expert', 'replica')
- up_grad: bfloat16 [64, 512, 3584], P('expert', 'replica')
- down_grad: bfloat16 [64, 512, 3584], P('expert', None, 'replica')
The draws below stay inside these ranges and needn't reach their ends.
Inputs may be any that keep to these rules, and one draw needn't show every extreme that they name: `expert_ids`: each row names 8 different experts. Among the 12 rows of one index of expert, no expert is named by more than 4 rows, a bound that some block reaches.
All inputs are finite; a program needn't handle non-finite values.
Results may differ from the reference program's by a relative error of at most 0.0075.
Values may be sent and summed in bfloat16 or wider, within the bound.
A program may use at most 64 MiB of HBM per device.

```python
import math
import jax
import jax.numpy as jnp
import numpy as np
from jax import lax

D = 3584
FF = 1024
TOPK = 8
TOK_DEV = 12
EXPERTS = 32
TOKENS = 768
MOST = 4
N_EXPERT = 64


def level_of(stream_key, shape, pieces, smallest, high):
    loudness, own = 1.0, jax.random.fold_in(stream_key, 6)
    for axis_at, parts in pieces:
        heights = jnp.exp(jax.random.uniform(jax.random.fold_in(own, axis_at), (parts,), jnp.float32, smallest / len(pieces), high / len(pieces)))
        loudness = loudness * jnp.repeat(heights, shape[axis_at] // parts).reshape([-1 if axis == axis_at else 1 for axis in range(len(shape))])
    return loudness


def routed_block(own_key, own, number, rows, number_of, top, reach, skew):
    ranking = jax.random.permutation(own_key, number_of)
    heavy_load, usual = shares(number_of, rows * top, reach, skew, True), shares(number_of, rows * top, reach, skew, False)
    places = jnp.arange(number_of)

    def named(sizes, turn):
        used = int((sizes > 0).sum())
        fixed = max(1, used // 4)
        shifted = fixed + (places - fixed + turn * (used - fixed)) % max(1, number_of - fixed)
        return jnp.zeros((number_of,), jnp.int32).at[ranking[jnp.where(places < fixed, places, shifted)]].set(jnp.asarray(sizes, jnp.int32))

    sizes = jnp.where(number % 4 == 0, named(heavy_load, number // 4), named(usual, number - number // 4 - 1))
    mixed = jax.random.permutation(jax.random.fold_in(own, 3), number_of)
    donor, taker = mixed[0:number_of // 2 * 2:2], mixed[1:number_of // 2 * 2:2]
    slack = jnp.minimum(sizes[donor] - 1, reach - sizes[taker]) // 2
    slack = jnp.where((donor == ranking[0]) | (taker == ranking[0]) | (sizes[taker] == 0), 0, jnp.maximum(slack, 0))
    shifted = jax.random.randint(jax.random.fold_in(own, 4), (number_of // 2,), 0, 1 << 20) % (slack + 1)
    sizes = sizes.at[donor].add(-shifted).at[taker].add(shifted)
    labels = jnp.searchsorted(jnp.cumsum(sizes), jnp.arange(rows * top), side="right").astype(jnp.int32)
    table = labels.reshape(top, rows).T
    table = table[jax.random.permutation(jax.random.fold_in(own, 1), rows)]
    turn = jax.random.randint(jax.random.fold_in(own, 2), (rows, 1), 0, top)
    return jnp.take_along_axis(table, (jnp.arange(top)[None, :] + turn) % top, axis=1)


def shares(amount, total, bound, slope, full):
    weights = [(1 << 20) // math.isqrt(grade ** slope) + 1 for grade in range(1, amount + 1)]
    largest = bound if full else min(bound, max(-(-total // amount), total * weights[0] // sum(weights)))
    least = 1 if total - largest >= amount - 1 else 0
    counts, rest = [largest] + [least] * (amount - 1), total - largest - least * (amount - 1)
    while rest > 0:
        candidates = [i for i in range(1, amount) if counts[i] < largest] or [i for i in range(1, amount) if counts[i] < bound]
        pool, budget = sum([weights[i] for i in candidates]), rest
        for i in candidates:
            addition = min(bound - counts[i], max(1, budget * weights[i] // pool), rest)
            counts[i] = counts[i] + addition
            rest = rest - addition
    return np.array(counts)


def gaussian(rng, extent, width, bound, split=(), kind=jnp.bfloat16):
    loudness = level_of(rng, extent, split, -0.22, 0.18) if split else 1.0
    entries = jax.random.normal(rng, extent, jnp.float32) * width * loudness
    return jnp.minimum(jnp.maximum(entries, -bound), bound).astype(kind)


def setup_inputs(seed: int = 0) -> dict:
    streams_of = jax.random.split(jax.random.key(seed), 8)
    tokens = gaussian(streams_of[0], (TOKENS, D), 1.0, 6.0, ((0, 64), (1, 8)))
    expert_ids_keys = jax.random.split(jax.random.fold_in(streams_of[1], 1), TOKENS // TOK_DEV)
    expert_ids_turns = jax.random.permutation(jax.random.fold_in(streams_of[1], 3), TOKENS // TOK_DEV)
    expert_ids = jax.vmap(lambda own, number: routed_block(jax.random.fold_in(streams_of[1], 2), own, number, TOK_DEV, EXPERTS, TOPK, MOST, 1))(expert_ids_keys, expert_ids_turns).reshape((TOKENS, TOPK))
    gate_values = jnp.clip(0.1 + 0.5 * jax.random.uniform(streams_of[2], (TOKENS, TOPK), jnp.float32) ** level_of(streams_of[2], (TOKENS, TOPK), ((0, 64),), -0.2, 0.2), 0.1, 0.6)
    gate_weight = gaussian(streams_of[3], (N_EXPERT, FF // 2, D), D ** -0.5, 0.09375, ((0, 64), (1, 8)))
    up_weight = gaussian(streams_of[4], (N_EXPERT, FF // 2, D), D ** -0.5, 0.09375, ((0, 64), (1, 8)))
    down_weight = gaussian(streams_of[5], (N_EXPERT, FF // 2, D), FF ** -0.5, 0.1875, ((0, 64), (2, 8)))
    out_grad = gaussian(streams_of[6], (TOKENS, D), 0.25, 1.5, ((0, 64), (1, 8)))
    return {"tokens": tokens, "expert_ids": expert_ids, "gate_values": gate_values, "gate_weight": gate_weight, "up_weight": up_weight, "down_weight": down_weight, "out_grad": out_grad}


def reference(tokens, expert_ids, gate_values, gate_weight, up_weight, down_weight, out_grad):
    pair_count = TOKENS * TOPK
    room_size = N_EXPERT * MOST
    flat_ids = expert_ids.reshape(pair_count).astype(jnp.int32)
    onehot = (flat_ids[:, None] == jnp.arange(EXPERTS, dtype=jnp.int32)[None, :]).astype(jnp.int32)
    rank_in = jnp.sum((jnp.cumsum(onehot, axis=0) - onehot) * onehot, axis=1).astype(jnp.int32)
    place = (flat_ids * room_size + rank_in).astype(jnp.int32)
    source_pair = jnp.zeros((EXPERTS * room_size,), jnp.int32).at[place].set(jnp.arange(pair_count, dtype=jnp.int32))
    filled = jnp.zeros((EXPERTS * room_size,), jnp.float32).at[place].set(1.0)
    token_index = (source_pair // TOPK).astype(jnp.int32).reshape(EXPERTS, room_size)
    live_mask = filled.reshape(EXPERTS, room_size)
    weight_of = gate_values.reshape(pair_count)[source_pair].reshape(EXPERTS, room_size)
    gate_mats = jnp.swapaxes(jnp.concatenate([gate_weight[0::2], gate_weight[1::2]], axis=1), 1, 2)
    up_mats = jnp.swapaxes(jnp.concatenate([up_weight[0::2], up_weight[1::2]], axis=1), 1, 2)
    down_mats = jnp.concatenate([down_weight[0::2], down_weight[1::2]], axis=1)

    def one_expert(operands):
        rows_index, row_live, row_weight, gate_mat, up_mat, down_mat = operands
        rows_in = jnp.where(row_live[:, None] > 0, tokens[rows_index], jnp.zeros((), tokens.dtype))
        pre_gate = jnp.dot(rows_in, gate_mat, preferred_element_type=jnp.float32)
        pre_up = jnp.dot(rows_in, up_mat, preferred_element_type=jnp.float32)
        sigma = jax.nn.sigmoid(pre_gate)
        activated = pre_gate * sigma
        slope_term = sigma * (1.0 + pre_gate * (1.0 - sigma))
        hidden = (activated * pre_up).astype(jnp.bfloat16)
        expert_out = jnp.dot(hidden, down_mat, preferred_element_type=jnp.float32).astype(jnp.bfloat16)
        cotangent = jnp.where(row_live[:, None] > 0, row_weight[:, None] * out_grad[rows_index].astype(jnp.float32), 0.0).astype(jnp.bfloat16)
        down_part = jnp.dot(hidden.T, cotangent, preferred_element_type=jnp.float32)
        hidden_grad = jnp.dot(cotangent, down_mat.T, preferred_element_type=jnp.float32)
        gate_act = (hidden_grad * pre_up * slope_term).astype(jnp.bfloat16)
        up_act = (hidden_grad * activated).astype(jnp.bfloat16)
        gate_part = jnp.dot(rows_in.T, gate_act, preferred_element_type=jnp.float32)
        up_part = jnp.dot(rows_in.T, up_act, preferred_element_type=jnp.float32)
        input_rows = (jnp.dot(gate_act, gate_mat.T, preferred_element_type=jnp.float32) + jnp.dot(up_act, up_mat.T, preferred_element_type=jnp.float32)).astype(jnp.bfloat16)
        return expert_out, input_rows, gate_part.astype(jnp.bfloat16), up_part.astype(jnp.bfloat16), down_part.astype(jnp.bfloat16)

    outs_all, inputs_all, gate_parts, up_parts, down_parts = lax.map(one_expert, (token_index, live_mask, weight_of, gate_mats, up_mats, down_mats))
    picked = outs_all.reshape(EXPERTS * room_size, D)[place].astype(jnp.float32).reshape(TOKENS, TOPK, D)
    moe_out = jnp.sum(picked * gate_values[:, :, None], axis=1).astype(jnp.bfloat16)
    picked_grad = inputs_all.reshape(EXPERTS * room_size, D)[place].astype(jnp.float32).reshape(TOKENS, TOPK, D)
    token_grad = jnp.sum(picked_grad, axis=1).astype(jnp.bfloat16)
    gate_grad = jnp.swapaxes(gate_parts, 1, 2).reshape(N_EXPERT, FF // 2, D)
    up_grad = jnp.swapaxes(up_parts, 1, 2).reshape(N_EXPERT, FF // 2, D)
    down_grad = down_parts.reshape(N_EXPERT, FF // 2, D)
    return moe_out, token_grad, gate_grad, up_grad, down_grad
```

```python
import functools

import jax
import jax.numpy as jnp
from jax import lax
from jax.experimental import pallas as pl
from jax.experimental.pallas import tpu as pltpu
from jax.sharding import PartitionSpec as P

MESH = pl.DeviceIdType.MESH
F32 = jnp.float32
BF16 = jnp.bfloat16
NN = (((1,), (0,)), ((), ()))
NT = (((1,), (1,)), ((), ()))
TN = (((0,), (0,)), ((), ()))


def mm(a, b, dims=NN):
    return lax.dot_general(a, b, dims, preferred_element_type=F32)


def split2(v):
    hi = v.astype(BF16)
    return hi, (v - hi.astype(F32)).astype(BF16)


def log2(n):
    return n.bit_length() - 1


def transposer(rows, outer, inner):
    r = lax.broadcasted_iota(jnp.int32, (rows, rows), 0)
    q = lax.broadcasted_iota(jnp.int32, (rows, rows), 1)
    hi = r >> (1 + log2(inner))
    lo = (r >> 1) & (inner - 1)
    want = (lo << (1 + log2(outer))) + (hi << 1) + (r & 1)
    return jnp.where(q == want, 1.0, 0.0).astype(BF16)


def kernel(
    nz,
    nd,
    ny,
    tok_ref,
    ids_ref,
    gv_ref,
    wg_ref,
    wu_ref,
    wd_ref,
    og_ref,
    moe_ref,
    tg_ref,
    gg_ref,
    ug_ref,
    dg_ref,
    tok16,
    og16,
    ids16,
    gv16,
    a_send,
    a_recv,
    b_send,
    dy_buf,
    x_all,
    w_raw,
    w_blk,
    wd_all,
    acc,
    dh_send,
    dh_recv,
    h_cat,
    rs_send,
    rs_recv,
    ret_send,
    ret_mid,
    ret_fwd,
    ret_recv,
    give,
    got,
    keep,
    give_d,
    got_d,
    keep_d,
    send_sem,
    recv_sem,
    local_sem,
):
    toks, top = ids_ref.shape
    feat = tok_ref.shape[1]
    hid = wg_ref.shape[0]
    rows = 2 * nz * nd
    half_rows = rows // 2
    hs = ny // 2
    me = lax.axis_index("expert")
    y = lax.axis_index("replica")
    c = lax.rem(me, 2)
    z = lax.rem(me // 2, nz)
    x = me // (2 * nz)
    d = 2 * x + c

    def at_z(k):
        t = lax.rem(z + k, nz)
        return t, {"expert": (x * nz + t) * 2 + c}

    def at_d(k):
        t = lax.rem(d + k, nd)
        return t, {"expert": ((t // 2) * nz + z) * 2 + lax.rem(t, 2)}

    def at_y(k):
        t = lax.rem(y + k + ny, ny)
        return t, {"replica": t}

    other = {"expert": (x * nz + z) * 2 + 1 - c}
    _, right = at_y(1)
    _, left = at_y(-1)

    used = []

    def remote(src, dst, dev):
        n = len(used)
        copy = pltpu.make_async_remote_copy(
            src_ref=src,
            dst_ref=dst,
            send_sem=send_sem.at[n],
            recv_sem=recv_sem.at[n],
            device_id=dev,
            device_id_type=MESH,
        )
        copy.start()
        used.append(copy)
        return copy

    barrier = pltpu.get_barrier_semaphore()
    partners = (
        [at_z(k)[1] for k in range(1, nz)]
        + [at_d(k)[1] for k in range(1, nd)]
        + [at_y(k)[1] for k in range(1, ny)]
    )
    for dev in partners:
        pl.semaphore_signal(barrier, inc=1, device_id=dev, device_id_type=MESH)

    own = [
        pltpu.make_async_copy(wd_ref, wd_all.at[:, 0:hid], local_sem.at[0]),
        pltpu.make_async_copy(wg_ref, w_raw.at[0], local_sem.at[1]),
        pltpu.make_async_copy(wu_ref, w_raw.at[2], local_sem.at[2]),
    ]
    for copy in own:
        copy.start()

    tok16[...] = jnp.zeros_like(tok16)
    og16[...] = jnp.zeros_like(og16)
    ids16[...] = jnp.full_like(ids16, -1)
    gv16[...] = jnp.zeros_like(gv16)
    tok16[0:toks, :] = tok_ref[...]
    og16[0:toks, :] = og_ref[...]
    ids16[0:toks, :] = ids_ref[...]
    gv16[0:toks, :] = gv_ref[...]
    lane = lax.broadcasted_iota(jnp.int32, (16, rows), 1)
    dd = (lane >> 1) & (nd - 1)
    expert = ((dd >> 1) << log2(nz)) + (lane >> (1 + log2(nd)))
    rank = (lane & 3).astype(F32)
    named = jnp.zeros((16, rows), F32)
    gates = jnp.zeros((16, rows), F32)
    for k in range(top):
        hit = ids16[:, k : k + 1] == expert
        named = jnp.where(hit, 1.0, named)
        gates = jnp.where(hit, gv16[:, k : k + 1], gates)
    t_row = lax.broadcasted_iota(jnp.int32, (16, 16), 0)
    t_col = lax.broadcasted_iota(jnp.int32, (16, 16), 1)
    before = jnp.where(t_col < t_row, 1.0, 0.0).astype(BF16)
    ahead = mm(before, named.astype(BF16))
    chosen = jnp.where(ahead == rank, named, 0.0)
    pick = chosen.astype(BF16)
    gate_hi, gate_lo = split2(gates * chosen)

    rows_x = mm(pick, tok16[...], TN).astype(BF16)
    a_send[0] = rows_x.reshape(nz, 2 * nd, feat)
    pl.semaphore_wait(barrier, len(partners))

    def stage_a(n):
        copies = []
        for k in range(1, nz):
            t, dev = at_z(k)
            copies.append(remote(a_send.at[n, t], a_recv.at[n, z], dev))
        a_recv[n, z] = a_send[n, z]
        return copies

    def stage_b(n, copies, dst):
        for copy in copies:
            copy.wait_recv()
        sorted_rows = mm(transposer(rows, nd, nz), a_recv[n].reshape(rows, feat))
        b_send[n] = sorted_rows.astype(BF16).reshape(nd, 2 * nz, feat)
        out = []
        for k in range(1, nd):
            t, dev = at_d(k)
            out.append(remote(b_send.at[n, t], dst.at[d], dev))
        dst[d] = b_send[n, d]
        return out

    a_x = stage_a(0)
    rows_dy = (mm(gate_hi, og16[...], TN) + mm(gate_lo, og16[...], TN)).astype(BF16)
    a_send[1] = rows_dy.reshape(nz, 2 * nd, feat)
    a_dy = stage_a(1)
    peer_d = remote(wd_ref, wd_all.at[:, hid : 2 * hid], other)
    peer_g = remote(wg_ref, w_raw.at[1], other)
    peer_u = remote(wu_ref, w_raw.at[3], other)

    def cut(j):
        for b in range(ny):
            w_blk[b, j * hid : (j + 1) * hid, :] = w_raw[j, :, b * feat : (b + 1) * feat]

    own[1].wait()
    cut(0)
    own[2].wait()
    cut(2)
    b_x = stage_b(0, a_x, x_all.at[y])
    b_dy = stage_b(1, a_dy, dy_buf)

    for copy in b_x:
        copy.wait_recv()
    nh = nd // 2

    def ring_send(s):
        br, bl = lax.rem(y - s + ny, ny), lax.rem(y + s, ny)
        if s < hs - 1:
            return remote(x_all.at[br], x_all.at[br], right), remote(
                x_all.at[bl], x_all.at[bl], left
            )
        return remote(x_all.at[br, 0:nh], x_all.at[br, 0:nh], right), remote(
            x_all.at[bl, nh:nd], x_all.at[bl, nh:nd], left
        )

    def rows_of(b):
        return x_all[b].reshape(rows, feat)

    ring = ring_send(0)

    for copy in b_dy:
        copy.wait_recv()
    own[0].wait()
    peer_d.wait_recv()
    dy = dy_buf[...].reshape(rows, feat)
    dh_copies = []
    for k in range(1, ny):
        t, dev = at_y(k)
        dh_send[t] = mm(dy, wd_all[t], NT).astype(BF16)
        dh_copies.append(remote(dh_send.at[t], dh_recv.at[y], dev))
    dh_own = mm(dy, wd_all[y], NT)

    peer_g.wait_recv()
    cut(1)
    peer_u.wait_recv()
    cut(3)
    acc[...] = mm(rows_of(y), w_blk[y], NT)
    for s in range(hs):
        for copy in ring:
            copy.wait_recv()
        if s + 1 < hs:
            ring = ring_send(s + 1)
            for b in (lax.rem(y - 1 - s + ny, ny), lax.rem(y + 1 + s, ny)):
                acc[...] += mm(rows_of(b), w_blk[b], NT)
        else:
            b = lax.rem(y + hs, ny)
            acc[...] += mm(rows_of(b), w_blk[b], NT)

    a = acc[:, 0 : 2 * hid]
    b = acc[:, 2 * hid : 4 * hid]
    sigma = 1.0 / (1.0 + jnp.exp(-a))
    act = a * sigma
    slope = sigma * (1.0 + a * (1.0 - sigma))
    span = pl.ds(pl.multiple_of(y * 2 * hid, 2 * hid), 2 * hid)
    h_cat[:, span] = (act * b).astype(BF16)
    h_copies = []
    for k in range(1, ny):
        _, dev = at_y(k)
        h_copies.append(remote(h_cat.at[:, span], h_cat.at[:, span], dev))
    dh = dh_own
    for k in range(1, ny):
        dh_copies[k - 1].wait_recv()
        dh = dh + dh_recv[lax.rem(y - k + ny, ny)].astype(F32)
    dab = jnp.concatenate(
        [(dh * b * slope).astype(BF16), (dh * act).astype(BF16)], axis=1
    )

    def part(b):
        return mm(dab, w_blk[lax.rem(b + 2 * ny, ny)])

    top_half, low_half = slice(0, half_rows), slice(half_rows, rows)

    def rs_start():
        p = part(y + hs).astype(BF16)
        rs_send[0, 0, top_half] = p[top_half]
        rs_send[1, 0, low_half] = p[low_half]
        return [
            remote(rs_send.at[0, 0, top_half], rs_recv.at[0, 0, top_half], right),
            remote(rs_send.at[1, 0, low_half], rs_recv.at[1, 0, low_half], left),
        ]

    def rs_step(s, before):
        after = []
        for way, dev, dest, half in (
            (0, right, y + hs - s, top_half),
            (1, left, y - hs + s, low_half),
        ):
            p = part(dest)
            before[way].wait_recv()
            if s == 1:
                rs_send[way, s] = p.astype(BF16)
                rs_send[way, s, half] = (
                    p[half] + rs_recv[way, 0, half].astype(F32)
                ).astype(BF16)
            else:
                rs_send[way, s] = (p + rs_recv[way, s - 1].astype(F32)).astype(BF16)
            after.append(remote(rs_send.at[way, s], rs_recv.at[way, s], dev))
        return after

    def back_b(n, value):
        ret_send[n] = value.astype(BF16).reshape(nd, 2 * nz, feat)
        out = []
        for k in range(1, nd):
            t, dev = at_d(k)
            out.append(remote(ret_send.at[n, t], ret_mid.at[n, d], dev))
        ret_mid[n, d] = ret_send[n, d]
        return out

    def back_a(n, copies):
        for copy in copies:
            copy.wait_recv()
        sorted_rows = mm(transposer(rows, nz, nd), ret_mid[n].reshape(rows, feat))
        ret_fwd[n] = sorted_rows.astype(BF16).reshape(nz, 2 * nd, feat)
        out = []
        for k in range(1, nz):
            t, dev = at_z(k)
            out.append(remote(ret_fwd.at[n, t], ret_recv.at[n, z], dev))
        ret_recv[n, z] = ret_fwd[n, z]
        return out

    rs = rs_start()
    rs = rs_step(1, rs)
    for copy in h_copies:
        copy.wait_recv()
    out = mm(h_cat[...], wd_all[...].reshape(ny * 2 * hid, feat))
    out_b = back_b(0, out)
    for b in range(ny):
        g = mm(dab, rows_of(b), TN)
        keep[b, 0:hid] = g[0:hid]
        keep[b, hid : 2 * hid] = g[2 * hid : 3 * hid]
        give[b, 0:hid] = g[hid : 2 * hid].astype(BF16)
        give[b, hid : 2 * hid] = g[3 * hid : 4 * hid].astype(BF16)
    give_copy = remote(give, got, other)
    if hs > 2:
        rs = rs_step(2, rs)
    out_a = back_a(0, out_b)
    for b in range(ny):
        g = mm(h_cat[:, b * 2 * hid : (b + 1) * 2 * hid], dy, TN)
        keep_d[b] = g[0:hid]
        give_d[b] = g[hid : 2 * hid].astype(BF16)
    give_d_copy = remote(give_d, got_d, other)
    for s in range(3, hs):
        rs = rs_step(s, rs)
    dx = part(y)
    for copy in rs:
        copy.wait_recv()
    dx = dx + rs_recv[0, hs - 1].astype(F32) + rs_recv[1, hs - 1].astype(F32)
    dx_b = back_b(1, dx)

    give_copy.wait_recv()
    for b in range(ny):
        span_b = slice(b * feat, (b + 1) * feat)
        gg_ref[:, span_b] = (keep[b, 0:hid] + got[b, 0:hid].astype(F32)).astype(BF16)
        ug_ref[:, span_b] = (
            keep[b, hid : 2 * hid] + got[b, hid : 2 * hid].astype(F32)
        ).astype(BF16)
    dx_a = back_a(1, dx_b)
    give_d_copy.wait_recv()
    dg_ref[...] = (keep_d[...] + got_d[...].astype(F32)).astype(BF16)

    for copy in out_a:
        copy.wait_recv()
    back = ret_recv[0].reshape(rows, feat)
    moe_ref[...] = (mm(gate_hi, back) + mm(gate_lo, back))[0:toks].astype(BF16)
    for copy in dx_a:
        copy.wait_recv()
    tg_ref[...] = mm(pick, ret_recv[1].reshape(rows, feat))[0:toks].astype(BF16)
    for copy in used:
        copy.wait_send()


def per_device(nz, tokens, ids, gate_values, gate_weight, up_weight, down_weight, out_grad):
    ne = lax.axis_size("expert")
    ny = lax.axis_size("replica")
    nd = ne // nz
    toks, feat = tokens.shape
    hid, width = gate_weight.shape[1:]
    rows = 2 * ne
    hs = ny // 2
    copies = 4 * (nz - 1) + 4 * (nd - 1) + 3 + 4 * hs + 2 * (ny - 1) + 2
    vmem = pl.BlockSpec(memory_space=pltpu.VMEM)
    hbm = pl.BlockSpec(memory_space=pl.ANY)
    moe, tg, gg, ug, dg = pl.pallas_call(
        functools.partial(kernel, nz, nd, ny),
        out_shape=(
            jax.ShapeDtypeStruct((toks, feat), BF16),
            jax.ShapeDtypeStruct((toks, feat), BF16),
            jax.ShapeDtypeStruct((hid, width), BF16),
            jax.ShapeDtypeStruct((hid, width), BF16),
            jax.ShapeDtypeStruct((ny, hid, feat), BF16),
        ),
        in_specs=[vmem, vmem, vmem, hbm, hbm, hbm, vmem],
        out_specs=(vmem,) * 5,
        scratch_shapes=[
            pltpu.VMEM((16, feat), BF16),
            pltpu.VMEM((16, feat), BF16),
            pltpu.VMEM((16, ids.shape[1]), jnp.int32),
            pltpu.VMEM((16, ids.shape[1]), F32),
            pltpu.VMEM((2, nz, 2 * nd, feat), BF16),
            pltpu.VMEM((2, nz, 2 * nd, feat), BF16),
            pltpu.VMEM((2, nd, 2 * nz, feat), BF16),
            pltpu.VMEM((nd, 2 * nz, feat), BF16),
            pltpu.VMEM((ny, nd, 2 * nz, feat), BF16),
            pltpu.VMEM((4, hid, width), BF16),
            pltpu.VMEM((ny, 4 * hid, feat), BF16),
            pltpu.VMEM((ny, 2 * hid, feat), BF16),
            pltpu.VMEM((rows, 4 * hid), F32),
            pltpu.VMEM((ny, rows, 2 * hid), BF16),
            pltpu.VMEM((ny, rows, 2 * hid), BF16),
            pltpu.VMEM((rows, ny * 2 * hid), BF16),
            pltpu.VMEM((2, hs, rows, feat), BF16),
            pltpu.VMEM((2, hs, rows, feat), BF16),
            pltpu.VMEM((2, nd, 2 * nz, feat), BF16),
            pltpu.VMEM((2, nd, 2 * nz, feat), BF16),
            pltpu.VMEM((2, nz, 2 * nd, feat), BF16),
            pltpu.VMEM((2, nz, 2 * nd, feat), BF16),
            pltpu.VMEM((ny, 2 * hid, feat), BF16),
            pltpu.VMEM((ny, 2 * hid, feat), BF16),
            pltpu.VMEM((ny, 2 * hid, feat), F32),
            pltpu.VMEM((ny, hid, feat), BF16),
            pltpu.VMEM((ny, hid, feat), BF16),
            pltpu.VMEM((ny, hid, feat), F32),
            pltpu.SemaphoreType.DMA((copies,)),
            pltpu.SemaphoreType.DMA((copies,)),
            pltpu.SemaphoreType.DMA((3,)),
        ],
        compiler_params=pltpu.CompilerParams(
            collective_id=0, has_side_effects=True, vmem_limit_bytes=48 * 1024 * 1024
        ),
    )(
        tokens,
        ids,
        gate_values,
        gate_weight[0],
        up_weight[0],
        down_weight[0].reshape(ny, hid, feat),
        out_grad,
    )
    return moe, tg, gg[None], ug[None], dg.reshape(1, ny * hid, feat)


def solution(mesh):
    nz = 8 if mesh.shape["expert"] == 64 else 2
    rows, whole = P("expert", "replica"), P("expert", None)
    units, slices = P("expert", "replica", None), P("expert", None, "replica")
    return jax.shard_map(
        functools.partial(per_device, nz),
        mesh=mesh,
        in_specs=(rows, whole, whole, units, units, slices, rows),
        out_specs=(rows, rows, units, units, slices),
        check_vma=False,
    )
```

```python
import functools

import jax
import jax.numpy as jnp
from jax import lax
from jax.experimental import pallas as pl
from jax.experimental.pallas import tpu as pltpu
from jax.sharding import PartitionSpec as P

MESH = pl.DeviceIdType.MESH
F32 = jnp.float32
BF16 = jnp.bfloat16
NN = (((1,), (0,)), ((), ()))
NT = (((1,), (1,)), ((), ()))
TN = (((0,), (0,)), ((), ()))


def mm(a, b, dims=NN):
    return lax.dot_general(a, b, dims, preferred_element_type=F32)


def split2(v):
    hi = v.astype(BF16)
    return hi, (v - hi.astype(F32)).astype(BF16)


def log2(n):
    return n.bit_length() - 1


def transposer(rows, outer, inner):
    r = lax.broadcasted_iota(jnp.int32, (rows, rows), 0)
    q = lax.broadcasted_iota(jnp.int32, (rows, rows), 1)
    hi = r >> (1 + log2(inner))
    lo = (r >> 1) & (inner - 1)
    want = (lo << (1 + log2(outer))) + (hi << 1) + (r & 1)
    return jnp.where(q == want, 1.0, 0.0).astype(BF16)


def kernel(
    nz,
    nd,
    ny,
    tok_ref,
    ids_ref,
    gv_ref,
    wg_ref,
    wu_ref,
    wd_ref,
    og_ref,
    moe_out,
    tg_out,
    gg_out,
    ug_out,
    dg_out,
    moe_ref,
    tg_ref,
    gg_ref,
    ug_ref,
    dg_ref,
    tok_in,
    og_in,
    ids_in,
    gv_in,
    tok16,
    og16,
    ids16,
    gv16,
    wd_raw,
    a_send,
    a_recv,
    b_send,
    dy_buf,
    x_all,
    w_raw,
    w_blk,
    wd_all,
    acc,
    dh_send,
    dh_recv,
    h_cat,
    rs_send,
    rs_recv,
    ret_send,
    ret_mid,
    ret_fwd,
    ret_recv,
    give,
    got,
    keep,
    give_d,
    got_d,
    keep_d,
    send_sem,
    recv_sem,
    local_sem,
):
    top, toks = ids_ref.shape
    feat = tok_ref.shape[1]
    hid = wg_ref.shape[0]
    rows = 2 * nz * nd
    half_rows = rows // 2
    hs = ny // 2
    width = 2 * hid
    me = lax.axis_index("expert")
    y = lax.axis_index("replica")
    c = lax.rem(me, 2)
    z = lax.rem(me // 2, nz)
    x = me // (2 * nz)
    d = 2 * x + c

    def at_z(k):
        t = lax.rem(z + k, nz)
        return t, {"expert": (x * nz + t) * 2 + c}

    def at_d(k):
        t = lax.rem(d + k, nd)
        return t, {"expert": ((t // 2) * nz + z) * 2 + lax.rem(t, 2)}

    def at_y(k):
        t = lax.rem(y + k + ny, ny)
        return t, {"replica": t}

    other = {"expert": (x * nz + z) * 2 + 1 - c}
    _, right = at_y(1)
    _, left = at_y(-1)

    used = []

    def remote(src, dst, dev):
        n = len(used)
        copy = pltpu.make_async_remote_copy(
            src_ref=src,
            dst_ref=dst,
            send_sem=send_sem.at[n],
            recv_sem=recv_sem.at[n],
            device_id=dev,
            device_id_type=MESH,
        )
        copy.start()
        used.append(copy)
        return copy

    barrier = pltpu.get_barrier_semaphore()
    partners = (
        [at_z(k)[1] for k in range(1, nz)]
        + [at_d(k)[1] for k in range(1, nd)]
        + [at_y(k)[1] for k in range(1, ny)]
    )
    for dev in partners:
        pl.semaphore_signal(barrier, inc=1, device_id=dev, device_id_type=MESH)

    small = [
        pltpu.make_async_copy(src, dst, local_sem.at[3 + n])
        for n, (src, dst) in enumerate(
            ((ids_ref, ids_in), (tok_ref, tok_in), (gv_ref, gv_in), (og_ref, og_in))
        )
    ]
    own = [
        pltpu.make_async_copy(wd_ref, wd_raw.at[0], local_sem.at[0]),
        pltpu.make_async_copy(wg_ref, w_raw.at[0], local_sem.at[1]),
        pltpu.make_async_copy(wu_ref, w_raw.at[2], local_sem.at[2]),
    ]
    for copy in small + own:
        copy.start()

    tok16[...] = jnp.zeros_like(tok16)
    og16[...] = jnp.zeros_like(og16)
    ids16[...] = jnp.full_like(ids16, -1)
    gv16[...] = jnp.zeros_like(gv16)
    for copy in small:
        copy.wait()
    tok16[0:toks, :] = tok_in[...]
    og16[0:toks, :] = og_in[...]
    ids16[:, 0:toks] = ids_in[...]
    gv16[:, 0:toks] = gv_in[...]
    slot = lax.broadcasted_iota(jnp.int32, (rows, 16), 0)
    dd = (slot >> 1) & (nd - 1)
    expert = ((dd >> 1) << log2(nz)) + (slot >> (1 + log2(nd)))
    rank = (slot & 3).astype(F32)
    named = jnp.zeros((rows, 16), F32)
    gates = jnp.zeros((rows, 16), F32)
    for k in range(top):
        hit = ids16[k : k + 1, :] == expert
        named = jnp.where(hit, 1.0, named)
        gates = jnp.where(hit, gv16[k : k + 1, :], gates)
    t_row = lax.broadcasted_iota(jnp.int32, (16, 16), 0)
    t_col = lax.broadcasted_iota(jnp.int32, (16, 16), 1)
    before = jnp.where(t_row < t_col, 1.0, 0.0).astype(BF16)
    ahead = mm(named.astype(BF16), before)
    chosen = jnp.where(ahead == rank, named, 0.0)
    pick = chosen.astype(BF16)
    gate_hi, gate_lo = split2(gates * chosen)

    rows_x = mm(pick, tok16[...]).astype(BF16)
    a_send[0] = rows_x.reshape(nz, 2 * nd, feat)
    pl.semaphore_wait(barrier, len(partners))

    def stage_a(n):
        copies = []
        for k in range(1, nz):
            t, dev = at_z(k)
            copies.append(remote(a_send.at[n, t], a_recv.at[n, z], dev))
        a_recv[n, z] = a_send[n, z]
        return copies

    def stage_b(n, copies, dst):
        for copy in copies:
            copy.wait_recv()
        sorted_rows = mm(transposer(rows, nd, nz), a_recv[n].reshape(rows, feat))
        b_send[n] = sorted_rows.astype(BF16).reshape(nd, 2 * nz, feat)
        out = []
        for k in range(1, nd):
            t, dev = at_d(k)
            out.append(remote(b_send.at[n, t], dst.at[d], dev))
        dst[d] = b_send[n, d]
        return out

    a_x = stage_a(0)
    rows_dy = (mm(gate_hi, og16[...]) + mm(gate_lo, og16[...])).astype(BF16)
    a_send[1] = rows_dy.reshape(nz, 2 * nd, feat)
    a_dy = stage_a(1)
    peer_d = remote(wd_ref, wd_raw.at[1], other)
    peer_g = remote(wg_ref, w_raw.at[1], other)
    peer_u = remote(wu_ref, w_raw.at[3], other)

    def cut(j):
        for b in range(ny):
            w_blk[b, j * hid : (j + 1) * hid, :] = w_raw[j, :, b * feat : (b + 1) * feat]

    own[1].wait()
    cut(0)
    own[2].wait()
    cut(2)
    b_x = stage_b(0, a_x, x_all.at[y])
    b_dy = stage_b(1, a_dy, dy_buf)

    nh = nd // 2
    chunks = (slice(0, nh), slice(nh, nd))
    ways = ((0, 1), (1, -1))
    arriving = {}

    def ring_send(s, ch, way, sign):
        b = lax.rem(y - sign * s + ny, ny)
        block = x_all.at[b, chunks[ch]]
        arriving[s, ch, way] = remote(block, block, at_y(sign)[1])

    def rows_of(b):
        return x_all[b].reshape(rows, feat)

    def ring_step(s):
        for ch in range(2):
            for way, sign in ways:
                arriving[s - 1, ch, way].wait_recv()
                if s < hs - 1 or ch == way:
                    ring_send(s, ch, way, sign)
        for way, sign in ways:
            b = lax.rem(y - sign * s + ny, ny)
            acc[...] += mm(rows_of(b), w_blk[b], NT)

    top_half, low_half = slice(0, half_rows), slice(half_rows, rows)
    halves = (top_half, low_half)

    def tree_far(part, send, recv):
        far = {}
        p = part(4).astype(BF16)
        for way, sign in ways:
            send[way, 0, halves[way]] = p[halves[way]]
            far[way, 0] = remote(
                send.at[way, 0, halves[way]], recv.at[way, 0, halves[way]], at_y(2 * sign)[1]
            )
        for way, sign in ways:
            send[way, 1] = part(3 * sign).astype(BF16)
            far[way, 1] = remote(send.at[way, 1], recv.at[way, 1], at_y(sign)[1])
        return far

    def tree_near(part, send, recv):
        near = []
        for way, sign in ways:
            send[way, 2] = part(sign).astype(BF16)
            near.append(remote(send.at[way, 2], recv.at[way, 2], at_y(sign)[1]))
        return near

    def tree_mid(part, send, recv, far):
        mid = []
        for way, sign in ways:
            p = part(2 * sign)
            far[way, 1].wait_recv()
            p = p + recv[way, 1].astype(F32)
            far[way, 0].wait_recv()
            half, rest = halves[way], halves[1 - way]
            send[way, 3, half] = (p[half] + recv[way, 0, half].astype(F32)).astype(BF16)
            send[way, 3, rest] = p[rest].astype(BF16)
            mid.append(remote(send.at[way, 3], recv.at[way, 3], at_y(2 * sign)[1]))
        return mid

    def tree_end(part, recv, near, mid):
        total = part(0)
        for way in range(2):
            near[way].wait_recv()
            total = total + recv[way, 2].astype(F32)
        for way in range(2):
            mid[way].wait_recv()
            total = total + recv[way, 3].astype(F32)
        return total

    def lanes(b):
        return pl.ds(pl.multiple_of(b * width, width), width)

    for copy in b_x:
        copy.wait_recv()
    for ch in range(2):
        for way, sign in ways:
            ring_send(0, ch, way, sign)

    own[0].wait()
    peer_d.wait_recv()
    for b in range(ny):
        span = slice(b * hid, (b + 1) * hid)
        wd_all[:, b * width : (b + 1) * width] = jnp.concatenate(
            [wd_raw[0, :, span], wd_raw[1, :, span]], axis=1
        )
    peer_g.wait_recv()
    cut(1)
    peer_u.wait_recv()
    cut(3)
    acc[...] = mm(rows_of(y), w_blk[y], NT)
    ring_step(1)

    for copy in b_dy:
        copy.wait_recv()
    dy = dy_buf[...].reshape(rows, feat)

    def dh_part(k):
        return mm(dy, wd_all[:, lanes(at_y(k)[0])])

    dh_far = tree_far(dh_part, dh_send, dh_recv)
    dh_near = tree_near(dh_part, dh_send, dh_recv)
    ring_step(2)
    dh_mid = tree_mid(dh_part, dh_send, dh_recv, dh_far)
    ring_step(3)
    for way in range(2):
        arriving[hs - 1, way, way].wait_recv()
    opposite = lax.rem(y + hs, ny)
    acc[...] += mm(rows_of(opposite), w_blk[opposite], NT)

    a = acc[:, 0:width]
    b = acc[:, width : 2 * width]
    sigma = 1.0 / (1.0 + jnp.exp(-a))
    act = a * sigma
    slope = sigma * (1.0 + a * (1.0 - sigma))
    h_cat[:, lanes(y)] = (act * b).astype(BF16)
    dh = tree_end(dh_part, dh_recv, dh_near, dh_mid)
    dab = jnp.concatenate(
        [(dh * b * slope).astype(BF16), (dh * act).astype(BF16)], axis=1
    )

    def dx_part(k):
        return mm(dab, w_blk[at_y(k)[0]])

    def h_send(dist, hops, half=None):
        out = []
        for way, sign in ways:
            b = lax.rem(y - sign * dist + ny, ny)
            block = h_cat.at[:, lanes(b)] if half is None else h_cat.at[halves[way], lanes(b)]
            out.append(remote(block, block, at_y(sign * hops)[1]))
        return out

    dx_far = tree_far(dx_part, rs_send, rs_recv)
    h_two = h_send(0, 2)
    h_one = h_send(0, 1)
    dx_near = tree_near(dx_part, rs_send, rs_recv)

    def back_b(n, value):
        ret_send[n] = value.astype(BF16).reshape(nd, 2 * nz, feat)
        out = []
        for k in range(1, nd):
            t, dev = at_d(k)
            out.append(remote(ret_send.at[n, t], ret_mid.at[n, d], dev))
        ret_mid[n, d] = ret_send[n, d]
        return out

    def back_a(n, copies):
        for copy in copies:
            copy.wait_recv()
        sorted_rows = mm(transposer(rows, nz, nd), ret_mid[n].reshape(rows, feat))
        ret_fwd[n] = sorted_rows.astype(BF16).reshape(nz, 2 * nd, feat)
        out = []
        for k in range(1, nz):
            t, dev = at_z(k)
            out.append(remote(ret_fwd.at[n, t], ret_recv.at[n, z], dev))
        ret_recv[n, z] = ret_fwd[n, z]
        return out

    for b in range(ny):
        g = mm(dab, rows_of(b), TN)
        keep[b, 0:hid] = g[0:hid]
        keep[b, hid : 2 * hid] = g[2 * hid : 3 * hid]
        give[b, 0:hid] = g[hid : 2 * hid].astype(BF16)
        give[b, hid : 2 * hid] = g[3 * hid : 4 * hid].astype(BF16)
    give_copy = remote(give, got, other)
    for copy in h_two:
        copy.wait_recv()
    h_three = h_send(2, 1)
    h_four = h_send(2, 2, half=True)
    dx_mid = tree_mid(dx_part, rs_send, rs_recv, dx_far)
    for copy in h_one + h_three + h_four:
        copy.wait_recv()
    out_b = back_b(0, mm(h_cat[...], wd_all[...], NT))
    g = mm(dy, h_cat[...], TN)
    for b in range(ny):
        span = slice(b * hid, (b + 1) * hid)
        keep_d[:, span] = g[:, b * width : b * width + hid]
        give_d[:, span] = g[:, b * width + hid : (b + 1) * width].astype(BF16)
    give_d_copy = remote(give_d, got_d, other)
    dx_b = back_b(1, tree_end(dx_part, rs_recv, dx_near, dx_mid))
    out_a = back_a(0, out_b)

    give_copy.wait_recv()
    for b in range(ny):
        span_b = slice(b * feat, (b + 1) * feat)
        gg_ref[:, span_b] = (keep[b, 0:hid] + got[b, 0:hid].astype(F32)).astype(BF16)
        ug_ref[:, span_b] = (
            keep[b, hid : 2 * hid] + got[b, hid : 2 * hid].astype(F32)
        ).astype(BF16)
    leaving = []

    def leave(src, dst):
        copy = pltpu.make_async_copy(src, dst, local_sem.at[7 + len(leaving)])
        copy.start()
        leaving.append(copy)

    leave(gg_ref, gg_out)
    leave(ug_ref, ug_out)
    dx_a = back_a(1, dx_b)
    give_d_copy.wait_recv()
    dg_ref[...] = (keep_d[...] + got_d[...].astype(F32)).astype(BF16)
    leave(dg_ref, dg_out)

    for copy in out_a:
        copy.wait_recv()
    back = ret_recv[0].reshape(rows, feat)
    moe_ref[...] = (mm(gate_hi, back, TN) + mm(gate_lo, back, TN))[0:toks].astype(BF16)
    leave(moe_ref, moe_out)
    for copy in dx_a:
        copy.wait_recv()
    tg_ref[...] = mm(pick, ret_recv[1].reshape(rows, feat), TN)[0:toks].astype(BF16)
    leave(tg_ref, tg_out)
    for copy in leaving:
        copy.wait()
    for copy in used:
        copy.wait_send()


def write_out(*refs):
    count = len(refs) // 3
    ins, outs, held = refs[:count], refs[count : 2 * count], refs[2 * count : 3 * count]
    sem = refs[-1]
    read = [pltpu.make_async_copy(i, h, sem.at[n]) for n, (i, h) in enumerate(zip(ins, held))]
    write = [
        pltpu.make_async_copy(h, o, sem.at[count + n])
        for n, (h, o) in enumerate(zip(held, outs))
    ]
    for copy in read:
        copy.start()
    for n in range(count):
        read[n].wait()
        write[n].start()
    for copy in write:
        copy.wait()


def per_device(nz, tokens, ids, gate_values, gate_weight, up_weight, down_weight, out_grad):
    ne = lax.axis_size("expert")
    ny = lax.axis_size("replica")
    nd = ne // nz
    toks, feat = tokens.shape
    top = ids.shape[1]
    hid, width = gate_weight.shape[1:]
    rows = 2 * ne
    hs = ny // 2
    copies = 4 * (nz - 1) + 4 * (nd - 1) + 5 + (4 * hs - 2) + 3 * 8
    hbm = pl.BlockSpec(memory_space=pltpu.HBM)
    moe, tg, gg, ug, dg = pl.pallas_call(
        functools.partial(kernel, nz, nd, ny),
        out_shape=(
            jax.ShapeDtypeStruct((toks, feat), BF16),
            jax.ShapeDtypeStruct((toks, feat), BF16),
            jax.ShapeDtypeStruct((hid, width), BF16),
            jax.ShapeDtypeStruct((hid, width), BF16),
            jax.ShapeDtypeStruct((feat, ny * hid), BF16),
        ),
        in_specs=[hbm] * 7,
        out_specs=(hbm,) * 5,
        scratch_shapes=[
            pltpu.VMEM((toks, feat), BF16),
            pltpu.VMEM((toks, feat), BF16),
            pltpu.VMEM((hid, width), BF16),
            pltpu.VMEM((hid, width), BF16),
            pltpu.VMEM((feat, ny * hid), BF16),
            pltpu.VMEM((toks, feat), BF16),
            pltpu.VMEM((toks, feat), BF16),
            pltpu.VMEM((top, toks), jnp.int32),
            pltpu.VMEM((top, toks), F32),
            pltpu.VMEM((16, feat), BF16),
            pltpu.VMEM((16, feat), BF16),
            pltpu.VMEM((top, 16), jnp.int32),
            pltpu.VMEM((top, 16), F32),
            pltpu.VMEM((2, feat, ny * hid), BF16),
            pltpu.VMEM((2, nz, 2 * nd, feat), BF16),
            pltpu.VMEM((2, nz, 2 * nd, feat), BF16),
            pltpu.VMEM((2, nd, 2 * nz, feat), BF16),
            pltpu.VMEM((nd, 2 * nz, feat), BF16),
            pltpu.VMEM((ny, nd, 2 * nz, feat), BF16),
            pltpu.VMEM((4, hid, width), BF16),
            pltpu.VMEM((ny, 4 * hid, feat), BF16),
            pltpu.VMEM((feat, 2 * ny * hid), BF16),
            pltpu.VMEM((rows, 4 * hid), F32),
            pltpu.VMEM((2, 4, rows, 2 * hid), BF16),
            pltpu.VMEM((2, 4, rows, 2 * hid), BF16),
            pltpu.VMEM((rows, ny * 2 * hid), BF16),
            pltpu.VMEM((2, 4, rows, feat), BF16),
            pltpu.VMEM((2, 4, rows, feat), BF16),
            pltpu.VMEM((2, nd, 2 * nz, feat), BF16),
            pltpu.VMEM((2, nd, 2 * nz, feat), BF16),
            pltpu.VMEM((2, nz, 2 * nd, feat), BF16),
            pltpu.VMEM((2, nz, 2 * nd, feat), BF16),
            pltpu.VMEM((ny, 2 * hid, feat), BF16),
            pltpu.VMEM((ny, 2 * hid, feat), BF16),
            pltpu.VMEM((ny, 2 * hid, feat), F32),
            pltpu.VMEM((feat, ny * hid), BF16),
            pltpu.VMEM((feat, ny * hid), BF16),
            pltpu.VMEM((feat, ny * hid), F32),
            pltpu.SemaphoreType.DMA((copies,)),
            pltpu.SemaphoreType.DMA((copies,)),
            pltpu.SemaphoreType.DMA((12,)),
        ],
        compiler_params=pltpu.CompilerParams(
            collective_id=0, has_side_effects=True, vmem_limit_bytes=60 * 1024 * 1024
        ),
    )(
        tokens,
        ids.T,
        gate_values.T,
        gate_weight[0],
        up_weight[0],
        down_weight[0].T,
        out_grad,
    )
    made = (moe, tg, gg, ug, dg)
    moe, tg, gg, ug, dg = pl.pallas_call(
        write_out,
        out_shape=tuple(jax.ShapeDtypeStruct(v.shape, v.dtype) for v in made),
        in_specs=[hbm] * 5,
        out_specs=(hbm,) * 5,
        scratch_shapes=[pltpu.VMEM(v.shape, v.dtype) for v in made]
        + [pltpu.SemaphoreType.DMA((10,))],
    )(*made)
    return moe, tg, gg[None], ug[None], dg.T[None]


def solution(mesh):
    nz = 8 if mesh.shape["expert"] == 64 else 2
    rows, whole = P("expert", "replica"), P("expert", None)
    units, slices = P("expert", "replica", None), P("expert", None, "replica")
    return jax.shard_map(
        functools.partial(per_device, nz),
        mesh=mesh,
        in_specs=(rows, whole, whole, units, units, slices, rows),
        out_specs=(rows, rows, units, units, slices),
        check_vma=False,
    )
```

```python
import functools

import jax
import jax.numpy as jnp
from jax import lax
from jax.experimental import pallas as pl
from jax.experimental.pallas import tpu as pltpu
from jax.sharding import PartitionSpec as P

MESH = pl.DeviceIdType.MESH
F32 = jnp.float32
BF16 = jnp.bfloat16
NN = (((1,), (0,)), ((), ()))
NT = (((1,), (1,)), ((), ()))
TN = (((0,), (0,)), ((), ()))


def mm(a, b, dims=NN):
    return lax.dot_general(a, b, dims, preferred_element_type=F32)


def split2(v):
    hi = v.astype(BF16)
    return hi, (v - hi.astype(F32)).astype(BF16)


def log2(n):
    return n.bit_length() - 1


def transposer(rows, outer, inner):
    r = lax.broadcasted_iota(jnp.int32, (rows, rows), 0)
    q = lax.broadcasted_iota(jnp.int32, (rows, rows), 1)
    hi = r >> (1 + log2(inner))
    lo = (r >> 1) & (inner - 1)
    want = (lo << (1 + log2(outer))) + (hi << 1) + (r & 1)
    return jnp.where(q == want, 1.0, 0.0).astype(BF16)


def kernel(
    nz,
    nd,
    ny,
    tok_ref,
    ids_ref,
    gv_ref,
    wg_ref,
    wu_ref,
    wd_ref,
    og_ref,
    moe_out,
    tg_out,
    gg_out,
    ug_out,
    dg_out,
    moe_ref,
    tg_ref,
    gg_ref,
    ug_ref,
    dg_ref,
    tok_in,
    og_in,
    ids_in,
    gv_in,
    tok16,
    og16,
    ids16,
    gv16,
    wd_raw,
    a_send,
    a_recv,
    b_send,
    x_buf,
    dy_buf,
    x_all,
    w_raw,
    w_blk,
    wd_all,
    acc,
    dh_send,
    dh_recv,
    h_cat,
    rs_send,
    rs_recv,
    ret_send,
    ret_mid,
    ret_fwd,
    ret_recv,
    give,
    got,
    keep,
    give_d,
    got_d,
    keep_d,
    send_sem,
    recv_sem,
    local_sem,
):
    top, toks = ids_ref.shape
    feat = tok_ref.shape[1]
    hid = wg_ref.shape[0]
    rows = 2 * nz * nd
    half_rows = rows // 2
    hs = ny // 2
    width = 2 * hid
    me = lax.axis_index("expert")
    y = lax.axis_index("replica")
    c = lax.rem(me, 2)
    z = lax.rem(me // 2, nz)
    x = me // (2 * nz)
    d = 2 * x + c

    def at_z(k):
        t = lax.rem(z + k, nz)
        return t, {"expert": (x * nz + t) * 2 + c}

    def at_d(k):
        t = lax.rem(d + k, nd)
        return t, {"expert": ((t // 2) * nz + z) * 2 + lax.rem(t, 2)}

    def at_y(k):
        t = lax.rem(y + k + ny, ny)
        return t, {"replica": t}

    other = {"expert": (x * nz + z) * 2 + 1 - c}
    _, right = at_y(1)
    _, left = at_y(-1)

    used = []

    def remote(src, dst, dev):
        n = len(used)
        copy = pltpu.make_async_remote_copy(
            src_ref=src,
            dst_ref=dst,
            send_sem=send_sem.at[n],
            recv_sem=recv_sem.at[n],
            device_id=dev,
            device_id_type=MESH,
        )
        copy.start()
        used.append(copy)
        return copy

    barrier = pltpu.get_barrier_semaphore()
    partners = (
        [at_z(k)[1] for k in range(1, nz)]
        + [at_d(k)[1] for k in range(1, nd)]
        + [at_y(k)[1] for k in range(1, ny)]
    )
    for dev in partners:
        pl.semaphore_signal(barrier, inc=1, device_id=dev, device_id_type=MESH)

    small = [
        pltpu.make_async_copy(src, dst, local_sem.at[3 + n])
        for n, (src, dst) in enumerate(
            ((ids_ref, ids_in), (tok_ref, tok_in), (gv_ref, gv_in), (og_ref, og_in))
        )
    ]
    own = [
        pltpu.make_async_copy(wd_ref, wd_raw.at[0], local_sem.at[0]),
        pltpu.make_async_copy(wg_ref, w_raw.at[0], local_sem.at[1]),
        pltpu.make_async_copy(wu_ref, w_raw.at[2], local_sem.at[2]),
    ]
    for copy in small + own:
        copy.start()

    tok16[...] = jnp.zeros_like(tok16)
    og16[...] = jnp.zeros_like(og16)
    ids16[...] = jnp.full_like(ids16, -1)
    gv16[...] = jnp.zeros_like(gv16)
    for copy in small:
        copy.wait()
    tok16[0:toks, :] = tok_in[...]
    og16[0:toks, :] = og_in[...]
    ids16[:, 0:toks] = ids_in[...]
    gv16[:, 0:toks] = gv_in[...]
    slot = lax.broadcasted_iota(jnp.int32, (rows, 16), 0)
    dd = (slot >> 1) & (nd - 1)
    expert = ((dd >> 1) << log2(nz)) + (slot >> (1 + log2(nd)))
    rank = (slot & 3).astype(F32)
    named = jnp.zeros((rows, 16), F32)
    gates = jnp.zeros((rows, 16), F32)
    for k in range(top):
        hit = ids16[k : k + 1, :] == expert
        named = jnp.where(hit, 1.0, named)
        gates = jnp.where(hit, gv16[k : k + 1, :], gates)
    t_row = lax.broadcasted_iota(jnp.int32, (16, 16), 0)
    t_col = lax.broadcasted_iota(jnp.int32, (16, 16), 1)
    before = jnp.where(t_row < t_col, 1.0, 0.0).astype(BF16)
    ahead = mm(named.astype(BF16), before)
    chosen = jnp.where(ahead == rank, named, 0.0)
    pick = chosen.astype(BF16)
    gate_hi, gate_lo = split2(gates * chosen)

    rows_x = mm(pick, tok16[...]).astype(BF16)
    a_send[0] = rows_x.reshape(nz, 2 * nd, feat)
    pl.semaphore_wait(barrier, len(partners))

    def stage_a(n):
        copies = []
        for k in range(1, nz):
            t, dev = at_z(k)
            copies.append(remote(a_send.at[n, t], a_recv.at[n, z], dev))
        a_recv[n, z] = a_send[n, z]
        return copies

    def stage_b(n, copies, dst):
        for copy in copies:
            copy.wait_recv()
        sorted_rows = mm(transposer(rows, nd, nz), a_recv[n].reshape(rows, feat))
        b_send[n] = sorted_rows.astype(BF16).reshape(nd, 2 * nz, feat)
        out = []
        for k in range(1, nd):
            t, dev = at_d(k)
            out.append(remote(b_send.at[n, t], dst.at[d], dev))
        dst[d] = b_send[n, d]
        return out

    a_x = stage_a(0)
    rows_dy = (mm(gate_hi, og16[...]) + mm(gate_lo, og16[...])).astype(BF16)
    a_send[1] = rows_dy.reshape(nz, 2 * nd, feat)
    peer_d = remote(wd_ref, wd_raw.at[1], other)
    peer_g = remote(wg_ref, w_raw.at[1], other)
    peer_u = remote(wu_ref, w_raw.at[3], other)

    def cut(j):
        for b in range(ny):
            w_blk[b, j * hid : (j + 1) * hid, :] = w_raw[j, :, b * feat : (b + 1) * feat]

    own[1].wait()
    cut(0)
    own[2].wait()
    cut(2)
    b_x = stage_b(0, a_x, x_buf)
    a_dy = stage_a(1)

    nh = half_rows // 2
    chunks = (slice(0, nh), slice(nh, half_rows))
    ways = ((0, 1), (1, -1))
    arriving = {}

    def ring_send(s, ch, way, sign):
        b = lax.rem(y - sign * s + ny, ny)
        block = x_all.at[b, chunks[ch]]
        arriving[s, ch, way] = remote(block, block, at_y(sign)[1])

    def pack(v):
        return jnp.concatenate([v[0:half_rows], v[half_rows:rows]], axis=1)

    def unpack(v):
        return jnp.concatenate([v[:, 0:feat], v[:, feat : 2 * feat]], axis=0)

    def rows_of(b):
        return unpack(x_all[b])

    def ring_step(s):
        for ch in range(2):
            for way, sign in ways:
                arriving[s - 1, ch, way].wait_recv()
                if s < hs - 1 or ch == way:
                    ring_send(s, ch, way, sign)
        for way, sign in ways:
            b = lax.rem(y - sign * s + ny, ny)
            acc[...] += mm(rows_of(b), w_blk[b], NT)

    def halves_of(n):
        return slice(0, n // 2), slice(n // 2, n)

    def tree_far(part, send, recv):
        halves = halves_of(send.shape[2])
        far = {}
        p = part(4).astype(BF16)
        for way, sign in ways:
            send[way, 0, halves[way]] = p[halves[way]]
            far[way, 0] = remote(
                send.at[way, 0, halves[way]], recv.at[way, 0, halves[way]], at_y(2 * sign)[1]
            )
        for way, sign in ways:
            send[way, 1] = part(3 * sign).astype(BF16)
            far[way, 1] = remote(send.at[way, 1], recv.at[way, 1], at_y(sign)[1])
        return far

    def tree_near(part, send, recv):
        near = []
        for way, sign in ways:
            send[way, 2] = part(sign).astype(BF16)
            near.append(remote(send.at[way, 2], recv.at[way, 2], at_y(sign)[1]))
        return near

    def tree_mid(part, send, recv, far):
        halves = halves_of(send.shape[2])
        mid = []
        for way, sign in ways:
            p = part(2 * sign)
            far[way, 1].wait_recv()
            p = p + recv[way, 1].astype(F32)
            far[way, 0].wait_recv()
            half, rest = halves[way], halves[1 - way]
            send[way, 3, half] = (p[half] + recv[way, 0, half].astype(F32)).astype(BF16)
            send[way, 3, rest] = p[rest].astype(BF16)
            mid.append(remote(send.at[way, 3], recv.at[way, 3], at_y(2 * sign)[1]))
        return mid

    def tree_end(part, recv, near, mid):
        total = part(0)
        for way in range(2):
            near[way].wait_recv()
            total = total + recv[way, 2].astype(F32)
        for way in range(2):
            mid[way].wait_recv()
            total = total + recv[way, 3].astype(F32)
        return total

    def lanes(b):
        return pl.ds(pl.multiple_of(b * width, width), width)

    for copy in b_x:
        copy.wait_recv()
    x_all[y] = pack(x_buf[...].reshape(rows, feat))
    for ch in range(2):
        for way, sign in ways:
            ring_send(0, ch, way, sign)
    b_dy = stage_b(1, a_dy, dy_buf)

    own[0].wait()
    peer_d.wait_recv()
    for b in range(ny):
        span = slice(b * hid, (b + 1) * hid)
        wd_all[:, b * width : (b + 1) * width] = jnp.concatenate(
            [wd_raw[0, :, span], wd_raw[1, :, span]], axis=1
        )
    peer_g.wait_recv()
    cut(1)
    peer_u.wait_recv()
    cut(3)
    acc[...] = mm(rows_of(y), w_blk[y], NT)
    ring_step(1)

    for copy in b_dy:
        copy.wait_recv()
    dy = dy_buf[...].reshape(rows, feat)

    def dh_part(k):
        return mm(dy, wd_all[:, lanes(at_y(k)[0])])

    dh_far = tree_far(dh_part, dh_send, dh_recv)
    dh_near = tree_near(dh_part, dh_send, dh_recv)
    ring_step(2)
    dh_mid = tree_mid(dh_part, dh_send, dh_recv, dh_far)
    ring_step(3)
    for way in range(2):
        arriving[hs - 1, way, way].wait_recv()
    opposite = lax.rem(y + hs, ny)
    acc[...] += mm(rows_of(opposite), w_blk[opposite], NT)

    a = acc[:, 0:width]
    b = acc[:, width : 2 * width]
    sigma = 1.0 / (1.0 + jnp.exp(-a))
    act = a * sigma
    slope = sigma * (1.0 + a * (1.0 - sigma))
    h_cat[:, lanes(y)] = (act * b).astype(BF16)

    def h_send(dist, hops, half=None):
        out = []
        for way, sign in ways:
            b = lax.rem(y - sign * dist + ny, ny)
            part = slice(0, rows) if half is None else halves_of(rows)[way]
            block = h_cat.at[part, lanes(b)]
            out.append(remote(block, block, at_y(sign * hops)[1]))
        return out

    h_two = h_send(0, 2)
    h_one = h_send(0, 1)
    dh = tree_end(dh_part, dh_recv, dh_near, dh_mid)
    dab = jnp.concatenate(
        [(dh * b * slope).astype(BF16), (dh * act).astype(BF16)], axis=1
    )

    def dx_part(k):
        return pack(mm(dab, w_blk[at_y(k)[0]]))

    dx_far = tree_far(dx_part, rs_send, rs_recv)
    dx_near = tree_near(dx_part, rs_send, rs_recv)

    def back_b(n, value):
        ret_send[n] = value.astype(BF16).reshape(nd, 2 * nz, feat)
        out = []
        for k in range(1, nd):
            t, dev = at_d(k)
            out.append(remote(ret_send.at[n, t], ret_mid.at[n, d], dev))
        ret_mid[n, d] = ret_send[n, d]
        return out

    def back_a(n, copies):
        for copy in copies:
            copy.wait_recv()
        sorted_rows = mm(transposer(rows, nz, nd), ret_mid[n].reshape(rows, feat))
        ret_fwd[n] = sorted_rows.astype(BF16).reshape(nz, 2 * nd, feat)
        out = []
        for k in range(1, nz):
            t, dev = at_z(k)
            out.append(remote(ret_fwd.at[n, t], ret_recv.at[n, z], dev))
        ret_recv[n, z] = ret_fwd[n, z]
        return out

    for b in range(ny):
        g = mm(dab, rows_of(b), TN)
        keep[b, 0:hid] = g[0:hid]
        keep[b, hid : 2 * hid] = g[2 * hid : 3 * hid]
        give[b, 0:hid] = g[hid : 2 * hid].astype(BF16)
        give[b, hid : 2 * hid] = g[3 * hid : 4 * hid].astype(BF16)
    give_copy = remote(give, got, other)
    for copy in h_two:
        copy.wait_recv()
    h_three = h_send(2, 1)
    h_four = h_send(2, 2, half=True)
    dx_mid = tree_mid(dx_part, rs_send, rs_recv, dx_far)
    for copy in h_one + h_three + h_four:
        copy.wait_recv()
    out_b = back_b(0, mm(h_cat[...], wd_all[...], NT))
    g = mm(dy, h_cat[...], TN)
    for b in range(ny):
        span = slice(b * hid, (b + 1) * hid)
        keep_d[:, span] = g[:, b * width : b * width + hid]
        give_d[:, span] = g[:, b * width + hid : (b + 1) * width].astype(BF16)
    give_d_copy = remote(give_d, got_d, other)
    dx_b = back_b(1, unpack(tree_end(dx_part, rs_recv, dx_near, dx_mid)))
    out_a = back_a(0, out_b)

    give_copy.wait_recv()
    for b in range(ny):
        span_b = slice(b * feat, (b + 1) * feat)
        gg_ref[:, span_b] = (keep[b, 0:hid] + got[b, 0:hid].astype(F32)).astype(BF16)
        ug_ref[:, span_b] = (
            keep[b, hid : 2 * hid] + got[b, hid : 2 * hid].astype(F32)
        ).astype(BF16)
    leaving = []

    def leave(src, dst):
        copy = pltpu.make_async_copy(src, dst, local_sem.at[7 + len(leaving)])
        copy.start()
        leaving.append(copy)

    leave(gg_ref, gg_out)
    leave(ug_ref, ug_out)
    dx_a = back_a(1, dx_b)
    give_d_copy.wait_recv()
    dg_ref[...] = (keep_d[...] + got_d[...].astype(F32)).astype(BF16)
    leave(dg_ref, dg_out)

    for copy in out_a:
        copy.wait_recv()
    back = ret_recv[0].reshape(rows, feat)
    moe_ref[...] = (mm(gate_hi, back, TN) + mm(gate_lo, back, TN))[0:toks].astype(BF16)
    leave(moe_ref, moe_out)
    for copy in dx_a:
        copy.wait_recv()
    tg_ref[...] = mm(pick, ret_recv[1].reshape(rows, feat), TN)[0:toks].astype(BF16)
    leave(tg_ref, tg_out)
    for copy in leaving:
        copy.wait()
    for copy in used:
        copy.wait_send()


def write_out(*refs):
    count = len(refs) // 3
    ins, outs, held = refs[:count], refs[count : 2 * count], refs[2 * count : 3 * count]
    sem = refs[-1]
    read = [pltpu.make_async_copy(i, h, sem.at[n]) for n, (i, h) in enumerate(zip(ins, held))]
    write = [
        pltpu.make_async_copy(h, o, sem.at[count + n])
        for n, (h, o) in enumerate(zip(held, outs))
    ]
    for copy in read:
        copy.start()
    for n in range(count):
        read[n].wait()
        write[n].start()
    for copy in write:
        copy.wait()


def per_device(nz, tokens, ids, gate_values, gate_weight, up_weight, down_weight, out_grad):
    ne = lax.axis_size("expert")
    ny = lax.axis_size("replica")
    nd = ne // nz
    toks, feat = tokens.shape
    top = ids.shape[1]
    hid, width = gate_weight.shape[1:]
    rows = 2 * ne
    hs = ny // 2
    copies = 4 * (nz - 1) + 4 * (nd - 1) + 5 + (4 * hs - 2) + 3 * 8
    hbm = pl.BlockSpec(memory_space=pltpu.HBM)
    moe, tg, gg, ug, dg = pl.pallas_call(
        functools.partial(kernel, nz, nd, ny),
        out_shape=(
            jax.ShapeDtypeStruct((toks, feat), BF16),
            jax.ShapeDtypeStruct((toks, feat), BF16),
            jax.ShapeDtypeStruct((hid, width), BF16),
            jax.ShapeDtypeStruct((hid, width), BF16),
            jax.ShapeDtypeStruct((feat, ny * hid), BF16),
        ),
        in_specs=[hbm] * 7,
        out_specs=(hbm,) * 5,
        scratch_shapes=[
            pltpu.VMEM((toks, feat), BF16),
            pltpu.VMEM((toks, feat), BF16),
            pltpu.VMEM((hid, width), BF16),
            pltpu.VMEM((hid, width), BF16),
            pltpu.VMEM((feat, ny * hid), BF16),
            pltpu.VMEM((toks, feat), BF16),
            pltpu.VMEM((toks, feat), BF16),
            pltpu.VMEM((top, toks), jnp.int32),
            pltpu.VMEM((top, toks), F32),
            pltpu.VMEM((16, feat), BF16),
            pltpu.VMEM((16, feat), BF16),
            pltpu.VMEM((top, 16), jnp.int32),
            pltpu.VMEM((top, 16), F32),
            pltpu.VMEM((2, feat, ny * hid), BF16),
            pltpu.VMEM((2, nz, 2 * nd, feat), BF16),
            pltpu.VMEM((2, nz, 2 * nd, feat), BF16),
            pltpu.VMEM((2, nd, 2 * nz, feat), BF16),
            pltpu.VMEM((nd, 2 * nz, feat), BF16),
            pltpu.VMEM((nd, 2 * nz, feat), BF16),
            pltpu.VMEM((ny, rows // 2, 2 * feat), BF16),
            pltpu.VMEM((4, hid, width), BF16),
            pltpu.VMEM((ny, 4 * hid, feat), BF16),
            pltpu.VMEM((feat, 2 * ny * hid), BF16),
            pltpu.VMEM((rows, 4 * hid), F32),
            pltpu.VMEM((2, 4, rows, 2 * hid), BF16),
            pltpu.VMEM((2, 4, rows, 2 * hid), BF16),
            pltpu.VMEM((rows, ny * 2 * hid), BF16),
            pltpu.VMEM((2, 4, rows // 2, 2 * feat), BF16),
            pltpu.VMEM((2, 4, rows // 2, 2 * feat), BF16),
            pltpu.VMEM((2, nd, 2 * nz, feat), BF16),
            pltpu.VMEM((2, nd, 2 * nz, feat), BF16),
            pltpu.VMEM((2, nz, 2 * nd, feat), BF16),
            pltpu.VMEM((2, nz, 2 * nd, feat), BF16),
            pltpu.VMEM((ny, 2 * hid, feat), BF16),
            pltpu.VMEM((ny, 2 * hid, feat), BF16),
            pltpu.VMEM((ny, 2 * hid, feat), F32),
            pltpu.VMEM((feat, ny * hid), BF16),
            pltpu.VMEM((feat, ny * hid), BF16),
            pltpu.VMEM((feat, ny * hid), F32),
            pltpu.SemaphoreType.DMA((copies,)),
            pltpu.SemaphoreType.DMA((copies,)),
            pltpu.SemaphoreType.DMA((12,)),
        ],
        compiler_params=pltpu.CompilerParams(
            collective_id=0, has_side_effects=True, vmem_limit_bytes=60 * 1024 * 1024
        ),
    )(
        tokens,
        ids.T,
        gate_values.T,
        gate_weight[0],
        up_weight[0],
        down_weight[0].T,
        out_grad,
    )
    made = (moe, tg, gg, ug, dg)
    moe, tg, gg, ug, dg = pl.pallas_call(
        write_out,
        out_shape=tuple(jax.ShapeDtypeStruct(v.shape, v.dtype) for v in made),
        in_specs=[hbm] * 5,
        out_specs=(hbm,) * 5,
        scratch_shapes=[pltpu.VMEM(v.shape, v.dtype) for v in made]
        + [pltpu.SemaphoreType.DMA((10,))],
    )(*made)
    return moe, tg, gg[None], ug[None], dg.T[None]


def solution(mesh):
    nz = 8 if mesh.shape["expert"] == 64 else 2
    rows, whole = P("expert", "replica"), P("expert", None)
    units, slices = P("expert", "replica", None), P("expert", None, "replica")
    return jax.shard_map(
        functools.partial(per_device, nz),
        mesh=mesh,
        in_specs=(rows, whole, whole, units, units, slices, rows),
        out_specs=(rows, rows, units, units, slices),
        check_vma=False,
    )
```

```python
import functools

import jax
import jax.numpy as jnp
from jax import lax
from jax.experimental import pallas as pl
from jax.experimental.pallas import tpu as pltpu
from jax.sharding import PartitionSpec as P

MESH = pl.DeviceIdType.MESH
F32 = jnp.float32
BF16 = jnp.bfloat16
NN = (((1,), (0,)), ((), ()))
NT = (((1,), (1,)), ((), ()))
TN = (((0,), (0,)), ((), ()))


def mm(a, b, dims=NN):
    return lax.dot_general(a, b, dims, preferred_element_type=F32)


def split2(v):
    hi = v.astype(BF16)
    return hi, (v - hi.astype(F32)).astype(BF16)


def log2(n):
    return n.bit_length() - 1


def transposer(rows, outer, inner):
    r = lax.broadcasted_iota(jnp.int32, (rows, rows), 0)
    q = lax.broadcasted_iota(jnp.int32, (rows, rows), 1)
    hi = r >> (1 + log2(inner))
    lo = (r >> 1) & (inner - 1)
    want = (lo << (1 + log2(outer))) + (hi << 1) + (r & 1)
    return jnp.where(q == want, 1.0, 0.0).astype(BF16)


def kernel(
    nz,
    nd,
    ny,
    tok_ref,
    ids_ref,
    gv_ref,
    wg_ref,
    wu_ref,
    wd_ref,
    og_ref,
    moe_out,
    tg_out,
    gg_out,
    ug_out,
    dg_out,
    moe_ref,
    tg_ref,
    gg_ref,
    ug_ref,
    dg_ref,
    tok_in,
    og_in,
    ids_in,
    gv_in,
    tok16,
    og16,
    ids16,
    gv16,
    wd_raw,
    a_send,
    a_recv,
    b_send,
    x_buf,
    dy_buf,
    x_all,
    w_raw,
    w_blk,
    wd_all,
    acc,
    dh_send,
    dh_recv,
    h_cat,
    rs_send,
    rs_recv,
    ret_send,
    ret_mid,
    ret_fwd,
    ret_recv,
    give,
    got,
    keep,
    give_d,
    got_d,
    keep_d,
    send_sem,
    recv_sem,
    local_sem,
):
    top, toks = ids_ref.shape
    feat = tok_ref.shape[1]
    hid = wg_ref.shape[0]
    rows = 2 * nz * nd
    half_rows = rows // 2
    hs = ny // 2
    width = 2 * hid
    me = lax.axis_index("expert")
    y = lax.axis_index("replica")
    c = lax.rem(me, 2)
    z = lax.rem(me // 2, nz)
    x = me // (2 * nz)
    d = 2 * x + c

    def at_z(k):
        t = lax.rem(z + k, nz)
        return t, {"expert": (x * nz + t) * 2 + c}

    def at_d(k):
        t = lax.rem(d + k, nd)
        return t, {"expert": ((t // 2) * nz + z) * 2 + lax.rem(t, 2)}

    def at_y(k):
        t = lax.rem(y + k + ny, ny)
        return t, {"replica": t}

    other = {"expert": (x * nz + z) * 2 + 1 - c}
    _, right = at_y(1)
    _, left = at_y(-1)

    used = []

    def remote(src, dst, dev):
        n = len(used)
        copy = pltpu.make_async_remote_copy(
            src_ref=src,
            dst_ref=dst,
            send_sem=send_sem.at[n],
            recv_sem=recv_sem.at[n],
            device_id=dev,
            device_id_type=MESH,
        )
        copy.start()
        used.append(copy)
        return copy

    barrier = pltpu.get_barrier_semaphore()
    partners = (
        [at_z(k)[1] for k in range(1, nz)]
        + [at_d(k)[1] for k in range(1, nd)]
        + [at_y(k)[1] for k in range(1, ny)]
    )
    for dev in partners:
        pl.semaphore_signal(barrier, inc=1, device_id=dev, device_id_type=MESH)

    small = [
        pltpu.make_async_copy(src, dst, local_sem.at[3 + n])
        for n, (src, dst) in enumerate(
            ((ids_ref, ids_in), (tok_ref, tok_in), (gv_ref, gv_in), (og_ref, og_in))
        )
    ]
    own = [
        pltpu.make_async_copy(wd_ref, wd_raw.at[0], local_sem.at[0]),
        pltpu.make_async_copy(wg_ref, w_raw.at[0], local_sem.at[1]),
        pltpu.make_async_copy(wu_ref, w_raw.at[2], local_sem.at[2]),
    ]
    for copy in small + own:
        copy.start()

    tok16[...] = jnp.zeros_like(tok16)
    og16[...] = jnp.zeros_like(og16)
    ids16[...] = jnp.full_like(ids16, -1)
    gv16[...] = jnp.zeros_like(gv16)
    for copy in small:
        copy.wait()
    tok16[0:toks, :] = tok_in[...]
    og16[0:toks, :] = og_in[...]
    ids16[:, 0:toks] = ids_in[...]
    gv16[:, 0:toks] = gv_in[...]
    slot = lax.broadcasted_iota(jnp.int32, (rows, 16), 0)
    dd = (slot >> 1) & (nd - 1)
    expert = ((dd >> 1) << log2(nz)) + (slot >> (1 + log2(nd)))
    rank = (slot & 3).astype(F32)
    named = jnp.zeros((rows, 16), F32)
    gates = jnp.zeros((rows, 16), F32)
    for k in range(top):
        hit = ids16[k : k + 1, :] == expert
        named = jnp.where(hit, 1.0, named)
        gates = jnp.where(hit, gv16[k : k + 1, :], gates)
    t_row = lax.broadcasted_iota(jnp.int32, (16, 16), 0)
    t_col = lax.broadcasted_iota(jnp.int32, (16, 16), 1)
    before = jnp.where(t_row < t_col, 1.0, 0.0).astype(BF16)
    ahead = mm(named.astype(BF16), before)
    chosen = jnp.where(ahead == rank, named, 0.0)
    pick = chosen.astype(BF16)
    gate_hi, gate_lo = split2(gates * chosen)

    rows_x = mm(pick, tok16[...]).astype(BF16)
    a_send[0] = rows_x.reshape(nz, 2 * nd, feat)
    pl.semaphore_wait(barrier, len(partners))

    def stage_a(n):
        copies = []
        for k in range(1, nz):
            t, dev = at_z(k)
            copies.append(remote(a_send.at[n, t], a_recv.at[n, z], dev))
        a_recv[n, z] = a_send[n, z]
        return copies

    def stage_b(n, copies, dst):
        for copy in copies:
            copy.wait_recv()
        sorted_rows = mm(transposer(rows, nd, nz), a_recv[n].reshape(rows, feat))
        b_send[n] = sorted_rows.astype(BF16).reshape(nd, 2 * nz, feat)
        out = []
        for k in range(1, nd):
            t, dev = at_d(k)
            out.append(remote(b_send.at[n, t], dst.at[d], dev))
        dst[d] = b_send[n, d]
        return out

    a_x = stage_a(0)
    rows_dy = (mm(gate_hi, og16[...]) + mm(gate_lo, og16[...])).astype(BF16)
    a_send[1] = rows_dy.reshape(nz, 2 * nd, feat)
    peer_d = remote(wd_ref, wd_raw.at[1], other)
    peer_g = remote(wg_ref, w_raw.at[1], other)
    peer_u = remote(wu_ref, w_raw.at[3], other)

    def cut(j):
        for b in range(ny):
            w_blk[b, j * hid : (j + 1) * hid, :] = w_raw[j, :, b * feat : (b + 1) * feat]

    own[1].wait()
    cut(0)
    own[2].wait()
    cut(2)
    b_x = stage_b(0, a_x, x_buf)
    a_dy = stage_a(1)

    nh = half_rows // 2
    chunks = (slice(0, nh), slice(nh, half_rows))
    ways = ((0, 1), (1, -1))
    arriving = {}

    def ring_send(s, ch, way, sign):
        b = lax.rem(y - sign * s + ny, ny)
        block = x_all.at[b, chunks[ch]]
        arriving[s, ch, way] = remote(block, block, at_y(sign)[1])

    def pack(v):
        return jnp.concatenate([v[0:half_rows], v[half_rows:rows]], axis=1)

    def unpack(v):
        return jnp.concatenate([v[:, 0:feat], v[:, feat : 2 * feat]], axis=0)

    def rows_of(b):
        return unpack(x_all[b])

    def ring_step(s):
        for ch in range(2):
            for way, sign in ways:
                arriving[s - 1, ch, way].wait_recv()
                if s < hs - 1 or ch == way:
                    ring_send(s, ch, way, sign)
        for way, sign in ways:
            b = lax.rem(y - sign * s + ny, ny)
            acc[...] += mm(rows_of(b), w_blk[b], NT)

    def halves_of(n):
        return slice(0, n // 2), slice(n // 2, n)

    def tree_far(part, send, recv):
        halves = halves_of(send.shape[2])
        far = {}
        p = part(4).astype(BF16)
        for way, sign in ways:
            send[way, 0, halves[way]] = p[halves[way]]
            far[way, 0] = remote(
                send.at[way, 0, halves[way]], recv.at[way, 0, halves[way]], at_y(2 * sign)[1]
            )
        for way, sign in ways:
            send[way, 1] = part(3 * sign).astype(BF16)
            far[way, 1] = remote(send.at[way, 1], recv.at[way, 1], at_y(sign)[1])
        return far

    def tree_near(part, send, recv):
        near = []
        for way, sign in ways:
            send[way, 2] = part(sign).astype(BF16)
            near.append(remote(send.at[way, 2], recv.at[way, 2], at_y(sign)[1]))
        return near

    def tree_mid(part, send, recv, far):
        halves = halves_of(send.shape[2])
        mid = []
        for way, sign in ways:
            p = part(2 * sign)
            far[way, 1].wait_recv()
            p = p + recv[way, 1].astype(F32)
            far[way, 0].wait_recv()
            half, rest = halves[way], halves[1 - way]
            send[way, 3, half] = (p[half] + recv[way, 0, half].astype(F32)).astype(BF16)
            send[way, 3, rest] = p[rest].astype(BF16)
            mid.append(remote(send.at[way, 3], recv.at[way, 3], at_y(2 * sign)[1]))
        return mid

    def tree_end(part, recv, near, mid):
        total = part(0)
        for way in range(2):
            near[way].wait_recv()
            total = total + recv[way, 2].astype(F32)
        for way in range(2):
            mid[way].wait_recv()
            total = total + recv[way, 3].astype(F32)
        return total

    def lanes(b):
        return pl.ds(pl.multiple_of(b * width, width), width)

    for copy in b_x:
        copy.wait_recv()
    x_all[y] = pack(x_buf[...].reshape(rows, feat))
    for ch in range(2):
        for way, sign in ways:
            ring_send(0, ch, way, sign)
    b_dy = stage_b(1, a_dy, dy_buf)

    own[0].wait()
    peer_d.wait_recv()
    for b in range(ny):
        span = slice(b * hid, (b + 1) * hid)
        wd_all[:, b * width : (b + 1) * width] = jnp.concatenate(
            [wd_raw[0, :, span], wd_raw[1, :, span]], axis=1
        )
    peer_g.wait_recv()
    cut(1)
    peer_u.wait_recv()
    cut(3)
    acc[...] = mm(rows_of(y), w_blk[y], NT)
    ring_step(1)

    for copy in b_dy:
        copy.wait_recv()
    dy = dy_buf[...].reshape(rows, feat)

    def dh_part(k):
        return mm(dy, wd_all[:, lanes(at_y(k)[0])])

    dh_far = tree_far(dh_part, dh_send, dh_recv)
    ring_step(2)
    dh_mid = tree_mid(dh_part, dh_send, dh_recv, dh_far)
    dh_near = tree_near(dh_part, dh_send, dh_recv)
    ring_step(3)
    for way in range(2):
        arriving[hs - 1, way, way].wait_recv()
    opposite = lax.rem(y + hs, ny)
    acc[...] += mm(rows_of(opposite), w_blk[opposite], NT)

    a = acc[:, 0:width]
    b = acc[:, width : 2 * width]
    sigma = 1.0 / (1.0 + jnp.exp(-a))
    act = a * sigma
    slope = sigma * (1.0 + a * (1.0 - sigma))
    h_cat[:, lanes(y)] = (act * b).astype(BF16)

    def h_send(dist, hops, half=None):
        out = []
        for way, sign in ways:
            b = lax.rem(y - sign * dist + ny, ny)
            part = slice(0, rows) if half is None else halves_of(rows)[way]
            block = h_cat.at[part, lanes(b)]
            out.append(remote(block, block, at_y(sign * hops)[1]))
        return out

    h_two = h_send(0, 2)
    dh = tree_end(dh_part, dh_recv, dh_near, dh_mid)
    dab = jnp.concatenate(
        [(dh * b * slope).astype(BF16), (dh * act).astype(BF16)], axis=1
    )

    def dx_part(k):
        return pack(mm(dab, w_blk[at_y(k)[0]]))

    dx_far = tree_far(dx_part, rs_send, rs_recv)
    h_one = h_send(0, 1)

    def back_b(n, value):
        ret_send[n] = value.astype(BF16).reshape(nd, 2 * nz, feat)
        out = []
        for k in range(1, nd):
            t, dev = at_d(k)
            out.append(remote(ret_send.at[n, t], ret_mid.at[n, d], dev))
        ret_mid[n, d] = ret_send[n, d]
        return out

    def back_a(n, copies):
        for copy in copies:
            copy.wait_recv()
        sorted_rows = mm(transposer(rows, nz, nd), ret_mid[n].reshape(rows, feat))
        ret_fwd[n] = sorted_rows.astype(BF16).reshape(nz, 2 * nd, feat)
        out = []
        for k in range(1, nz):
            t, dev = at_z(k)
            out.append(remote(ret_fwd.at[n, t], ret_recv.at[n, z], dev))
        ret_recv[n, z] = ret_fwd[n, z]
        return out

    for b in range(ny):
        g = mm(dab, rows_of(b), TN)
        keep[b, 0:hid] = g[0:hid]
        keep[b, hid : 2 * hid] = g[2 * hid : 3 * hid]
        give[b, 0:hid] = g[hid : 2 * hid].astype(BF16)
        give[b, hid : 2 * hid] = g[3 * hid : 4 * hid].astype(BF16)
    give_copy = remote(give, got, other)
    for copy in h_two:
        copy.wait_recv()
    h_three = h_send(2, 1)
    h_four = h_send(2, 2, half=True)
    dx_mid = tree_mid(dx_part, rs_send, rs_recv, dx_far)
    dx_near = tree_near(dx_part, rs_send, rs_recv)
    for copy in h_one + h_three + h_four:
        copy.wait_recv()
    out_b = back_b(0, mm(h_cat[...], wd_all[...], NT))
    dx_b = back_b(1, unpack(tree_end(dx_part, rs_recv, dx_near, dx_mid)))
    out_a = back_a(0, out_b)
    g = mm(dy, h_cat[...], TN)
    for b in range(ny):
        span = slice(b * hid, (b + 1) * hid)
        keep_d[:, span] = g[:, b * width : b * width + hid]
        give_d[:, span] = g[:, b * width + hid : (b + 1) * width].astype(BF16)
    give_d_copy = remote(give_d, got_d, other)

    give_copy.wait_recv()
    for b in range(ny):
        span_b = slice(b * feat, (b + 1) * feat)
        gg_ref[:, span_b] = (keep[b, 0:hid] + got[b, 0:hid].astype(F32)).astype(BF16)
        ug_ref[:, span_b] = (
            keep[b, hid : 2 * hid] + got[b, hid : 2 * hid].astype(F32)
        ).astype(BF16)
    leaving = []

    def leave(src, dst):
        copy = pltpu.make_async_copy(src, dst, local_sem.at[7 + len(leaving)])
        copy.start()
        leaving.append(copy)

    leave(gg_ref, gg_out)
    leave(ug_ref, ug_out)
    dx_a = back_a(1, dx_b)
    give_d_copy.wait_recv()
    dg_ref[...] = (keep_d[...] + got_d[...].astype(F32)).astype(BF16)
    leave(dg_ref, dg_out)

    for copy in out_a:
        copy.wait_recv()
    back = ret_recv[0].reshape(rows, feat)
    moe_ref[...] = (mm(gate_hi, back, TN) + mm(gate_lo, back, TN))[0:toks].astype(BF16)
    leave(moe_ref, moe_out)
    for copy in dx_a:
        copy.wait_recv()
    tg_ref[...] = mm(pick, ret_recv[1].reshape(rows, feat), TN)[0:toks].astype(BF16)
    leave(tg_ref, tg_out)
    for copy in leaving:
        copy.wait()
    for copy in used:
        copy.wait_send()


def write_out(*refs):
    count = len(refs) // 3
    ins, outs, held = refs[:count], refs[count : 2 * count], refs[2 * count : 3 * count]
    sem = refs[-1]
    read = [pltpu.make_async_copy(i, h, sem.at[n]) for n, (i, h) in enumerate(zip(ins, held))]
    write = [
        pltpu.make_async_copy(h, o, sem.at[count + n])
        for n, (h, o) in enumerate(zip(held, outs))
    ]
    for copy in read:
        copy.start()
    for n in range(count):
        read[n].wait()
        write[n].start()
    for copy in write:
        copy.wait()


def per_device(nz, tokens, ids, gate_values, gate_weight, up_weight, down_weight, out_grad):
    ne = lax.axis_size("expert")
    ny = lax.axis_size("replica")
    nd = ne // nz
    toks, feat = tokens.shape
    top = ids.shape[1]
    hid, width = gate_weight.shape[1:]
    rows = 2 * ne
    hs = ny // 2
    copies = 4 * (nz - 1) + 4 * (nd - 1) + 5 + (4 * hs - 2) + 3 * 8
    hbm = pl.BlockSpec(memory_space=pltpu.HBM)
    moe, tg, gg, ug, dg = pl.pallas_call(
        functools.partial(kernel, nz, nd, ny),
        out_shape=(
            jax.ShapeDtypeStruct((toks, feat), BF16),
            jax.ShapeDtypeStruct((toks, feat), BF16),
            jax.ShapeDtypeStruct((hid, width), BF16),
            jax.ShapeDtypeStruct((hid, width), BF16),
            jax.ShapeDtypeStruct((feat, ny * hid), BF16),
        ),
        in_specs=[hbm] * 7,
        out_specs=(hbm,) * 5,
        scratch_shapes=[
            pltpu.VMEM((toks, feat), BF16),
            pltpu.VMEM((toks, feat), BF16),
            pltpu.VMEM((hid, width), BF16),
            pltpu.VMEM((hid, width), BF16),
            pltpu.VMEM((feat, ny * hid), BF16),
            pltpu.VMEM((toks, feat), BF16),
            pltpu.VMEM((toks, feat), BF16),
            pltpu.VMEM((top, toks), jnp.int32),
            pltpu.VMEM((top, toks), F32),
            pltpu.VMEM((16, feat), BF16),
            pltpu.VMEM((16, feat), BF16),
            pltpu.VMEM((top, 16), jnp.int32),
            pltpu.VMEM((top, 16), F32),
            pltpu.VMEM((2, feat, ny * hid), BF16),
            pltpu.VMEM((2, nz, 2 * nd, feat), BF16),
            pltpu.VMEM((2, nz, 2 * nd, feat), BF16),
            pltpu.VMEM((2, nd, 2 * nz, feat), BF16),
            pltpu.VMEM((nd, 2 * nz, feat), BF16),
            pltpu.VMEM((nd, 2 * nz, feat), BF16),
            pltpu.VMEM((ny, rows // 2, 2 * feat), BF16),
            pltpu.VMEM((4, hid, width), BF16),
            pltpu.VMEM((ny, 4 * hid, feat), BF16),
            pltpu.VMEM((feat, 2 * ny * hid), BF16),
            pltpu.VMEM((rows, 4 * hid), F32),
            pltpu.VMEM((2, 4, rows, 2 * hid), BF16),
            pltpu.VMEM((2, 4, rows, 2 * hid), BF16),
            pltpu.VMEM((rows, ny * 2 * hid), BF16),
            pltpu.VMEM((2, 4, rows // 2, 2 * feat), BF16),
            pltpu.VMEM((2, 4, rows // 2, 2 * feat), BF16),
            pltpu.VMEM((2, nd, 2 * nz, feat), BF16),
            pltpu.VMEM((2, nd, 2 * nz, feat), BF16),
            pltpu.VMEM((2, nz, 2 * nd, feat), BF16),
            pltpu.VMEM((2, nz, 2 * nd, feat), BF16),
            pltpu.VMEM((ny, 2 * hid, feat), BF16),
            pltpu.VMEM((ny, 2 * hid, feat), BF16),
            pltpu.VMEM((ny, 2 * hid, feat), F32),
            pltpu.VMEM((feat, ny * hid), BF16),
            pltpu.VMEM((feat, ny * hid), BF16),
            pltpu.VMEM((feat, ny * hid), F32),
            pltpu.SemaphoreType.DMA((copies,)),
            pltpu.SemaphoreType.DMA((copies,)),
            pltpu.SemaphoreType.DMA((12,)),
        ],
        compiler_params=pltpu.CompilerParams(
            collective_id=0, has_side_effects=True, vmem_limit_bytes=60 * 1024 * 1024
        ),
    )(
        tokens,
        ids.T,
        gate_values.T,
        gate_weight[0],
        up_weight[0],
        down_weight[0].T,
        out_grad,
    )
    made = (moe, tg, gg, ug, dg)
    moe, tg, gg, ug, dg = pl.pallas_call(
        write_out,
        out_shape=tuple(jax.ShapeDtypeStruct(v.shape, v.dtype) for v in made),
        in_specs=[hbm] * 5,
        out_specs=(hbm,) * 5,
        scratch_shapes=[pltpu.VMEM(v.shape, v.dtype) for v in made]
        + [pltpu.SemaphoreType.DMA((10,))],
    )(*made)
    return moe, tg, gg[None], ug[None], dg.T[None]


def solution(mesh):
    nz = 8 if mesh.shape["expert"] == 64 else 2
    rows, whole = P("expert", "replica"), P("expert", None)
    units, slices = P("expert", "replica", None), P("expert", None, "replica")
    return jax.shard_map(
        functools.partial(per_device, nz),
        mesh=mesh,
        in_specs=(rows, whole, whole, units, units, slices, rows),
        out_specs=(rows, rows, units, units, slices),
        check_vma=False,
    )
```
